32 devices in a mesh: lat: 8 (over z, x), lon: 4 (over y, core).
Axes of the slice: x: 2, y: 2, z: 4, core: 2. Of those that a mesh axis runs over, the one named last changes fastest.
Arguments:
- fields: bfloat16 [32, 720, 2, 512], P('lat', 'lon'), may hold values from -6 to 6
- coeffs: float32 [1024, 3], replicated, may hold values from -1.2 to 1.2
- entries: int32 [8, 4, 4, 128], replicated, may hold values from -3 to 1023, as said below
- band_info: int32 [8, 3], replicated, may hold values from 0 to 4, as said below
- conv_weight: bfloat16 [1536, 512], replicated, may hold values from -0.15625 to 0.15625
- mix_weight: bfloat16 [512, 512], replicated, may hold values from -0.25 to 0.25
Outputs:
- mixed: bfloat16 [32, 720, 2, 512], P('lat', 'lon')
The draws below stay inside these ranges and needn't reach their ends.
Inputs may be any that keep to these rules, and one draw needn't show every extreme that they name: `entries`: in band b's list every in row lies in b's own rows b * 4 to (b + 1) * 4 - 1, every out row differs from its in row by at most 3, shifts are 0 to 6 and filter rows 0 to 1023. `band_info`: count is 1 to 4 and equals 4 in the first and the last band; ext_lo and ext_hi are 0 to 3 and both equal 3 in bands 0, 1 and the last band.
All inputs are finite; a program needn't handle non-finite values.
Results may differ from the reference program's by a relative error of at most 0.0065.
Values may be sent and summed in bfloat16 or wider, within the bound.
A program may use at most 128 MiB of HBM per device.

```python
import jax
import jax.numpy as jnp
from jax import lax

CHANNELS = 512
NLON = 720
MEMBERS = 2
BASIS = 3
SHIFTS = 7
OVERHANG = 3
BLOCKS = 4
FILTERS = 1024
LAT_DEV = 4
NBANDS = 8
NLAT = 32


def draw_entries(key, part):
    keys = jax.random.split(jax.random.fold_in(key, 11), 4)
    shape = (NBANDS, BLOCKS, 128)
    band_list = jnp.arange(NBANDS, dtype=jnp.int32)[:, None, None]
    in_rows = band_list * LAT_DEV + jax.random.randint(keys[0], shape, 0, LAT_DEV, dtype=jnp.int32)
    deltas = jax.random.randint(keys[1], shape, -OVERHANG, OVERHANG + 1, dtype=jnp.int32)
    out_rows = in_rows + deltas
    shifts = jax.random.randint(keys[2], shape, 0, SHIFTS, dtype=jnp.int32)
    filter_rows = jax.random.randint(keys[3], shape, 0, FILTERS, dtype=jnp.int32)
    return jnp.stack([out_rows, in_rows, shifts, filter_rows], axis=2).astype(jnp.int32)


def draw_band_info(key, part):
    keys = jax.random.split(jax.random.fold_in(key, 23), 2)
    band_list = jnp.arange(NBANDS, dtype=jnp.int32)
    distance = jnp.minimum(band_list, NBANDS - 1 - band_list)
    halfway = max(1, (NBANDS - 1) // 2)
    spare = jax.random.randint(keys[0], (NBANDS,), 0, BLOCKS, dtype=jnp.int32)
    counts = BLOCKS - spare * distance // halfway
    extents = jax.random.randint(keys[1], (NBANDS, 2), 0, OVERHANG + 1, dtype=jnp.int32)
    pinned = (band_list == 0) | (band_list == 1) | (band_list == NBANDS - 1)
    extents = jnp.where(pinned[:, None], OVERHANG, extents)
    return jnp.concatenate([counts[:, None], extents], axis=1).astype(jnp.int32)


def levels(own_key, dims, shards, smallest, high):
    level = 1.0
    for dim, parts in shards:
        steps = jax.random.uniform(jax.random.fold_in(jax.random.fold_in(own_key, 6), dim), (parts,), jnp.float32, smallest / len(shards), high / len(shards))
        level = level * jnp.repeat(jnp.exp(steps), dims[dim] // parts).reshape((-1,) + (1,) * (len(dims) - 1 - dim))
    return level


def bell_draw(own_key, shape, width, bound, cuts=(), kind=jnp.bfloat16):
    factor_of = levels(own_key, shape, cuts, -0.22, 0.18) if cuts else 1.0
    array = jax.random.normal(own_key, shape, jnp.float32) * width * factor_of
    return jnp.minimum(jnp.maximum(array, -bound), bound).astype(kind)


def setup_inputs(seed: int = 0) -> dict:
    splits = jax.random.split(jax.random.key(seed), 7)
    fields = bell_draw(splits[0], (NLAT, NLON, MEMBERS, CHANNELS), 1.0, 6.0, ((0, 8), (1, 4)))
    coeffs = bell_draw(splits[1], (FILTERS, BASIS), 0.2, 1.2, (), jnp.float32)
    entries = draw_entries(jax.random.fold_in(splits[6], 71), 0)
    band_info = draw_band_info(jax.random.fold_in(splits[6], 71), 0)
    conv_weight = bell_draw(splits[4], (BASIS * CHANNELS, CHANNELS), (BASIS * CHANNELS) ** -0.5, 0.15625)
    mix_weight = bell_draw(splits[5], (CHANNELS, CHANNELS), CHANNELS ** -0.5, 0.25)
    return {"fields": fields, "coeffs": coeffs, "entries": entries, "band_info": band_info, "conv_weight": conv_weight, "mix_weight": mix_weight}


def band_coupling(entries, band_meta, coeffs, band_index, out_start, out_count, in_start, in_count, band_rows, grid_rows):
    nbands = entries.shape[0]
    clamped = jnp.clip(band_index, 0, nbands - 1).astype(jnp.int32)
    listed = lax.dynamic_index_in_dim(entries, clamped, 0, keepdims=False)
    meta = lax.dynamic_index_in_dim(band_meta, clamped, 0, keepdims=False)
    blocks = listed.shape[0]
    flattened = jnp.transpose(listed, (1, 0, 2)).reshape(4, blocks * 128)
    out_rows = flattened[0]
    in_rows = flattened[1]
    shifts = flattened[2]
    filter_rows = flattened[3]
    block_ids = jnp.arange(blocks * 128, dtype=jnp.int32) // 128
    own_rel = out_rows - clamped * band_rows
    usable = (band_index >= 0) & (band_index < nbands) & (block_ids < meta[0])
    usable = usable & (own_rel >= -meta[1]) & (own_rel < band_rows + meta[2])
    usable = usable & (out_rows >= 0) & (out_rows < grid_rows)
    filter_pick = (filter_rows[:, None] == jnp.arange(coeffs.shape[0], dtype=jnp.int32)[None, :]).astype(jnp.float32)
    values = jnp.dot(filter_pick, coeffs, precision=lax.Precision.HIGHEST, preferred_element_type=jnp.float32)
    values = values * usable[:, None].astype(jnp.float32)
    out_hit = ((out_rows - out_start)[:, None] == jnp.arange(out_count, dtype=jnp.int32)[None, :]).astype(jnp.float32)
    basis = coeffs.shape[1]
    left_side = (out_hit[:, :, None] * values[:, None, :]).reshape(blocks * 128, out_count * basis)
    nshift = SHIFTS
    in_hit = ((shifts * in_count + in_rows - in_start)[:, None] == jnp.arange(nshift * in_count, dtype=jnp.int32)[None, :]).astype(jnp.float32)
    return jnp.dot(left_side.T, in_hit, precision=lax.Precision.HIGHEST, preferred_element_type=jnp.float32)


def reference(fields, coeffs, entries, band_info, conv_weight, mix_weight):
    kernel = conv_weight.reshape(BASIS, CHANNELS, CHANNELS).astype(jnp.float32)
    mixing = mix_weight.astype(jnp.float32)
    out_count = LAT_DEV + 2 * OVERHANG

    def band_rows_of(band_index):
        clamped = jnp.clip(band_index, 0, NBANDS - 1).astype(jnp.int32)
        band_fields = lax.dynamic_slice_in_dim(fields, (clamped * LAT_DEV).astype(jnp.int32), LAT_DEV, 0)
        coupling = band_coupling(entries, band_info, coeffs, band_index, band_index * LAT_DEV - OVERHANG, out_count,
                                 band_index * LAT_DEV, LAT_DEV, LAT_DEV, NLAT).astype(jnp.bfloat16)
        flattened = band_fields.reshape(LAT_DEV, NLON, MEMBERS * CHANNELS)
        stacked = jnp.concatenate([jnp.roll(flattened, offset, axis=1) for offset in range(SHIFTS)], axis=0)
        stacked = stacked.reshape(SHIFTS * LAT_DEV, NLON * MEMBERS * CHANNELS)
        result = jnp.dot(coupling, stacked, preferred_element_type=jnp.float32)
        return result.reshape(out_count, BASIS, NLON, MEMBERS, CHANNELS)

    def finish(middle):
        features = middle.astype(jnp.bfloat16).astype(jnp.float32)
        combined = jnp.einsum('lkomc,kcd->lomd', features, kernel)
        activated = jax.nn.gelu(combined, approximate=True).astype(jnp.bfloat16).astype(jnp.float32)
        return jnp.einsum('lomc,cd->lomd', activated, mixing).astype(jnp.bfloat16)

    def advance(carry, band_index):
        pending_mid, pending_up = carry
        extended = band_rows_of(band_index)
        finished = pending_mid + jnp.pad(extended[:OVERHANG], ((LAT_DEV - OVERHANG, 0), (0, 0), (0, 0), (0, 0), (0, 0)))
        emitted = finish(finished)
        new_mid = extended[OVERHANG:OVERHANG + LAT_DEV] + jnp.pad(pending_up, ((0, LAT_DEV - OVERHANG), (0, 0), (0, 0), (0, 0), (0, 0)))
        new_up = extended[OVERHANG + LAT_DEV:]
        return (new_mid, new_up), emitted

    start_mid = jnp.zeros((LAT_DEV, BASIS, NLON, MEMBERS, CHANNELS), jnp.float32)
    start_up = jnp.zeros((OVERHANG, BASIS, NLON, MEMBERS, CHANNELS), jnp.float32)
    band_list = jnp.arange(NBANDS + 1, dtype=jnp.int32)
    carry_out, emitted_all = lax.scan(advance, (start_mid, start_up), band_list)
    return emitted_all[1:].reshape(NLAT, NLON, MEMBERS, CHANNELS)
```

```python
import functools

import jax
import jax.numpy as jnp
from jax import lax
from jax.experimental import pallas as pl
from jax.experimental.pallas import tpu as pltpu
from jax.sharding import PartitionSpec as P

CHANNELS = 512
MEMBERS = 2
BASIS = 3
SHIFTS = 7
OVERHANG = 3
LAT_DEV = 4
PAIR = 2 * LAT_DEV
ROWS_IN = PAIR + 2 * OVERHANG
TILE = 16
PIECE = 48
MESH = pl.DeviceIdType.MESH


def dot(a, b, dims=(((1,), (0,)), ((), ()))):
    return lax.dot_general(a, b, dims, preferred_element_type=jnp.float32)


def split3(x):
    high = x.astype(jnp.bfloat16).astype(jnp.float32)
    rest = x - high
    middle = rest.astype(jnp.bfloat16).astype(jnp.float32)
    low = (rest - middle).astype(jnp.bfloat16).astype(jnp.float32)
    return jnp.concatenate([high, middle, low], axis=0)


def pair_coupling(band, pair, nbands, entries_ref, info_ref, coeffs3):
    inside = ((band >= 0) & (band < nbands)).astype(jnp.int32)
    clamped = jnp.clip(band, 0, nbands - 1)
    listed = entries_ref[clamped]
    blocks = listed.shape[0]
    queue = blocks * 128
    out_rows, in_rows, shifts, filters = (
        jnp.concatenate([listed[j, f : f + 1, :] for j in range(blocks)], axis=1) for f in range(4)
    )
    count = info_ref[clamped, 0] * inside
    low = info_ref[clamped, 1]
    high = info_ref[clamped, 2]
    block_ids = lax.shift_right_logical(lax.broadcasted_iota(jnp.int32, (1, queue), 1), 7)
    relative = out_rows - clamped * LAT_DEV
    live = (block_ids < count) & (relative >= -low) & (relative < LAT_DEV + high)
    live = live & (out_rows >= 0) & (out_rows < nbands * LAT_DEV)
    table = coeffs3.shape[1]
    pick = lax.broadcasted_iota(jnp.int32, (table, queue), 0) == filters
    parts = dot(coeffs3, pick.astype(jnp.float32).astype(jnp.bfloat16))
    values = parts[0:8] + parts[8:16] + parts[16:24]
    out_hit = lax.broadcasted_iota(jnp.int32, (PAIR, queue), 0) == out_rows - pair * PAIR
    hit = jnp.where(out_hit & live, 1.0, 0.0)
    left = jnp.concatenate([hit * values[k : k + 1] for k in range(BASIS)], axis=0)
    in_index = shifts * 16 + in_rows - (pair * PAIR - OVERHANG)
    in_hit = lax.broadcasted_iota(jnp.int32, (SHIFTS * 16, queue), 0) == in_index
    in_hit = in_hit.astype(jnp.float32).astype(jnp.bfloat16)
    return dot(split3(left).astype(jnp.bfloat16), in_hit, (((1,), (1,)), ((), ())))


def toeplitz(coupling):
    shape = (BASIS * PAIR * TILE, ROWS_IN * 2 * TILE)
    source = lax.broadcasted_iota(jnp.int32, (shape[0], BASIS * PAIR), 0) // TILE
    spread = source == lax.broadcasted_iota(jnp.int32, (shape[0], BASIS * PAIR), 1)
    tall = dot(spread.astype(jnp.float32).astype(jnp.bfloat16), coupling).astype(jnp.bfloat16)
    row = lax.broadcasted_iota(jnp.int32, shape, 0) & (TILE - 1)
    column = lax.broadcasted_iota(jnp.int32, shape, 1) & (2 * TILE - 1)
    distance = row + TILE - column
    wide = (SHIFTS * 16, shape[1])
    own = lax.broadcasted_iota(jnp.int32, wide, 0)
    target = lax.shift_right_logical(lax.broadcasted_iota(jnp.int32, wide, 1), 5)
    total = jnp.zeros(shape, jnp.float32)
    for shift in range(SHIFTS):
        place = (own == target + shift * 16).astype(jnp.float32).astype(jnp.bfloat16)
        total = jnp.where(distance == 2 * shift, dot(tall, place), total)
    return total.astype(jnp.bfloat16)


def kernel(
    nlat,
    nlon,
    half,
    field_ref,
    coeffs_ref,
    entries_ref,
    info_ref,
    conv_ref,
    mix_ref,
    out_ref,
    ext,
    halo,
    head,
    spread,
    features,
    result,
    tail_send,
    tail_recv,
    in_send,
    in_recv,
    up_send,
    up_recv,
    down_send,
    down_recv,
    back_send,
    back_recv,
):
    pieces = half // PIECE
    lat = lax.axis_index("lat")
    lon = lax.axis_index("lon")
    pair = lat // 2
    side = lat - 2 * pair
    other = 1 - side
    partner = (lat + 1 - 2 * side, lon)
    above = (lat + 2, lon)
    below = (lat - 2, lon)
    has_above = lat + 2 < nlat
    has_below = lat >= 2
    east = (lat, lax.rem(lon + 1, nlon))
    west = (lat, lax.rem(lon + nlon - 1, nlon))

    barrier = pltpu.get_barrier_semaphore()
    for device in (partner, east, west):
        pl.semaphore_signal(barrier, inc=1, device_id=device, device_id_type=MESH)

    @pl.when(has_above)
    def _():
        pl.semaphore_signal(barrier, inc=1, device_id=above, device_id_type=MESH)

    @pl.when(has_below)
    def _():
        pl.semaphore_signal(barrier, inc=1, device_id=below, device_id_type=MESH)

    pl.semaphore_wait(barrier, 3 + has_above.astype(jnp.int32) + has_below.astype(jnp.int32))

    def remote(source, target, send, recv, device):
        return pltpu.make_async_remote_copy(
            src_ref=source,
            dst_ref=target,
            send_sem=send,
            recv_sem=recv,
            device_id=device,
            device_id_type=MESH,
        )

    last = field_ref.shape[1] - TILE
    tail_copy = remote(field_ref.at[:, pl.ds(last, TILE)], halo, tail_send, tail_recv, east)
    tail_copy.start()
    here = OVERHANG + LAT_DEV * side
    there = OVERHANG + LAT_DEV * other

    def inward(j):
        start = pl.multiple_of(other * half + TILE + PIECE * j, TILE)
        return remote(
            field_ref.at[:, pl.ds(start, PIECE)],
            ext.at[pl.ds(here, LAT_DEV), pl.ds(TILE + PIECE * j, PIECE)],
            in_send.at[j],
            in_recv.at[j],
            partner,
        )

    inward(0).start()
    window = pl.multiple_of(side * half + TILE, TILE)
    ext[pl.ds(here, LAT_DEV), pl.ds(TILE, half)] = field_ref[:, pl.ds(window, half)]

    @pl.when(jnp.logical_not(has_below))
    def _():
        ext[pl.ds(0, OVERHANG)] = jnp.zeros((OVERHANG, half + TILE, CHANNELS), jnp.bfloat16)

    @pl.when(jnp.logical_not(has_above))
    def _():
        ext[pl.ds(OVERHANG + PAIR, OVERHANG)] = jnp.zeros((OVERHANG, half + TILE, CHANNELS), jnp.bfloat16)

    tail_copy.wait()
    middle = field_ref[:, pl.ds(half, TILE)]
    arrived = halo[...]
    head[...] = jnp.where(side == 0, middle, arrived)
    ext[pl.ds(here, LAT_DEV), pl.ds(0, TILE)] = jnp.where(side == 0, arrived, middle)
    head_copy = remote(
        head,
        ext.at[pl.ds(here, LAT_DEV), pl.ds(0, TILE)],
        in_send.at[pieces],
        in_recv.at[pieces],
        partner,
    )
    head_copy.start()
    for j in range(1, pieces):
        inward(j).start()

    coeffs3 = split3(coeffs_ref[...]).astype(jnp.bfloat16)
    terms = 0.0
    for step in range(-1, 3):
        terms = terms + pair_coupling(2 * pair + step, pair, nlat, entries_ref, info_ref, coeffs3)
    rows = BASIS * PAIR
    coupling = terms[0:rows] + terms[rows : 2 * rows] + terms[2 * rows : 3 * rows]
    spread[...] = toeplitz(coupling.astype(jnp.bfloat16))

    def columns(j):
        return pl.ds(0, TILE + PIECE) if j == 0 else pl.ds(TILE + PIECE * j, PIECE)

    def upward(j):
        return remote(
            ext.at[pl.ds(PAIR, OVERHANG), columns(j)],
            ext.at[pl.ds(0, OVERHANG), columns(j)],
            up_send.at[j],
            up_recv.at[j],
            above,
        )

    def downward(j):
        return remote(
            ext.at[pl.ds(OVERHANG, OVERHANG), columns(j)],
            ext.at[pl.ds(OVERHANG + PAIR, OVERHANG), columns(j)],
            down_send.at[j],
            down_recv.at[j],
            below,
        )

    def outward(j):
        start = pl.multiple_of(side * half + PIECE * j, TILE)
        return remote(
            result.at[pl.ds(LAT_DEV * other, LAT_DEV), pl.ds(PIECE * j, PIECE)],
            out_ref.at[:, pl.ds(start, PIECE)],
            back_send.at[j],
            back_recv.at[j],
            partner,
        )

    def forward(j):
        inward(j).wait()
        if j == 0:
            head_copy.wait()

        @pl.when(has_above)
        def _():
            upward(j).start()

        @pl.when(has_below)
        def _():
            downward(j).start()

    def compute(j):
        @pl.when(has_above)
        def _():
            upward(j).wait_send()
            downward(j).wait_recv()

        @pl.when(has_below)
        def _():
            downward(j).wait_send()
            upward(j).wait_recv()

        filters = spread[...]
        group = PAIR * TILE
        blocks = PIECE // TILE
        for b in range(blocks):
            window_rows = ext[:, pl.ds(PIECE * j + TILE * b, 2 * TILE)]
            block = dot(filters, window_rows.reshape(ROWS_IN * 2 * TILE, CHANNELS)).astype(jnp.bfloat16)
            for k in range(BASIS):
                features[pl.ds(group * b, group), pl.ds(CHANNELS * k, CHANNELS)] = block[group * k : group * (k + 1)]
        combined = dot(features[...], conv_ref[...])
        activated = jax.nn.gelu(combined, approximate=True).astype(jnp.bfloat16)
        mixed = dot(activated, mix_ref[...]).astype(jnp.bfloat16)
        for b in range(blocks):
            part = mixed[group * b : group * (b + 1)].reshape(PAIR, TILE, CHANNELS)
            result[:, pl.ds(PIECE * j + TILE * b, TILE)] = part
        outward(j).start()
        start = pl.multiple_of(side * half + PIECE * j, TILE)
        out_ref[:, pl.ds(start, PIECE)] = result[pl.ds(LAT_DEV * side, LAT_DEV), pl.ds(PIECE * j, PIECE)]

    forward(0)
    for j in range(pieces):
        if j + 1 < pieces:
            forward(j + 1)
        compute(j)
    for j in range(pieces):
        outward(j).wait()


def shards(nlat, nlon, fields, coeffs, entries, band_info, conv_weight, mix_weight):
    rows = fields.shape[1] * MEMBERS
    half = -(-rows // (2 * PIECE)) * PIECE
    pieces = half // PIECE
    flat = fields.reshape(LAT_DEV, rows, CHANNELS)
    field = jnp.concatenate(
        [
            jnp.zeros((LAT_DEV, TILE, CHANNELS), fields.dtype),
            flat,
            jnp.zeros((LAT_DEV, 2 * half - rows, CHANNELS), fields.dtype),
            flat[:, rows - TILE :],
        ],
        axis=1,
    )
    table = jnp.pad(coeffs.T, ((0, 8 - BASIS), (0, 0)))
    vmem = pl.BlockSpec(memory_space=pltpu.VMEM)
    smem = pl.BlockSpec(memory_space=pltpu.SMEM)
    dma = pltpu.SemaphoreType.DMA
    bf16 = jnp.bfloat16
    out = pl.pallas_call(
        functools.partial(kernel, nlat, nlon, half),
        out_shape=jax.ShapeDtypeStruct((LAT_DEV, 2 * half, CHANNELS), bf16),
        in_specs=[vmem, vmem, vmem, smem, vmem, vmem],
        out_specs=vmem,
        scratch_shapes=[
            pltpu.VMEM((ROWS_IN, TILE + half, CHANNELS), bf16),
            pltpu.VMEM((LAT_DEV, TILE, CHANNELS), bf16),
            pltpu.VMEM((LAT_DEV, TILE, CHANNELS), bf16),
            pltpu.VMEM((BASIS * PAIR * TILE, ROWS_IN * 2 * TILE), bf16),
            pltpu.VMEM((PAIR * PIECE, BASIS * CHANNELS), bf16),
            pltpu.VMEM((PAIR, half, CHANNELS), bf16),
            dma,
            dma,
            dma((pieces + 1,)),
            dma((pieces + 1,)),
            dma((pieces,)),
            dma((pieces,)),
            dma((pieces,)),
            dma((pieces,)),
            dma((pieces,)),
            dma((pieces,)),
        ],
        compiler_params=pltpu.CompilerParams(
            collective_id=0, has_side_effects=True, vmem_limit_bytes=48 * 1024 * 1024
        ),
    )(field, table, entries, band_info, conv_weight, mix_weight)
    return out[:, :rows].reshape(fields.shape)


def solution(mesh):
    in_specs = (P("lat", "lon", None, None), P(), P(), P(), P(), P())
    out_specs = P("lat", "lon", None, None)
    body = functools.partial(shards, mesh.shape["lat"], mesh.shape["lon"])
    return jax.shard_map(body, mesh=mesh, in_specs=in_specs, out_specs=out_specs, check_vma=False)
```
